256 devices in a mesh: prow: 8 (over y, core), pcol: 32 (over x, z).
Axes of the slice: x: 4, y: 4, z: 8, core: 2. Of those that a mesh axis runs over, the one named last changes fastest.
Arguments:
- matrix: bfloat16 [28672, 16384], P('prow', 'pcol'), may hold values from -6 to 6
- u_inverse: float32 [2, 512, 512], replicated, may hold values from -0.02 to 0.2, as said below
- l_inverse: float32 [2, 512, 512], replicated, may hold values from -0.02 to 0.2, as said below
Outputs:
- factored: bfloat16 [28672, 16384], P('prow', 'pcol')
The draws below stay inside these ranges and needn't reach their ends.
Inputs may be any that keep to these rules, and one draw needn't show every extreme that they name: u_inverse[p] is upper triangular with positive diagonal. l_inverse[p] is lower triangular with positive diagonal.
All inputs are finite; a program needn't handle non-finite values.
Results may differ from the reference program's by a relative error of at most 0.008.
Values may be sent and summed in bfloat16 or wider, within the bound.
No kernel may reach another device: no remote copies, remote signals or barrier semaphores. Data moves between devices by JAX's collectives and lax.ppermute only.
A program may use at most 64 MiB of HBM per device.

```python
import jax
import jax.numpy as jnp
from jax import lax

NB = 512
PANELS = 2
RB = 7
ORDER = 28672
WCOLS = 16384
N_PROW = 8


def draw_u_inverse(key, part):
    first, second = jax.random.split(jax.random.fold_in(key, 11))
    diagonal = jax.random.uniform(first, (PANELS, NB), jnp.float32, 0.1, 0.2)
    spread = jax.random.uniform(second, (PANELS, NB, NB), jnp.float32, -0.02, 0.02)
    return jnp.triu(spread, 1) + diagonal[:, :, None] * jnp.eye(NB, dtype=jnp.float32)[None]


def draw_l_inverse(key, part):
    first, second = jax.random.split(jax.random.fold_in(key, 23))
    diagonal = jax.random.uniform(first, (PANELS, NB), jnp.float32, 0.1, 0.2)
    spread = jax.random.uniform(second, (PANELS, NB, NB), jnp.float32, -0.02, 0.02)
    return jnp.tril(spread, -1) + diagonal[:, :, None] * jnp.eye(NB, dtype=jnp.float32)[None]


def block_scale(rng, extent, cuts, smallest, largest):
    loudness = 1.0
    for dim, blocks in cuts:
        steps = jax.random.uniform(jax.random.fold_in(jax.random.fold_in(rng, 6), dim), (blocks,), jnp.float32, smallest / len(cuts), largest / len(cuts))
        loudness = loudness * jnp.repeat(jnp.exp(steps), extent[dim] // blocks).reshape((-1,) + (1,) * (len(extent) - 1 - dim))
    return loudness


def scatter_about(stream_key, shape, scale, most, cuts=(), held_as=jnp.bfloat16):
    loudness = block_scale(stream_key, shape, cuts, -0.22, 0.18) if cuts else 1.0
    values = jax.random.normal(stream_key, shape, jnp.float32) * scale * loudness
    return jnp.minimum(jnp.maximum(values, -most), most).astype(held_as)


def setup_inputs(seed: int = 0) -> dict:
    arg_keys = jax.random.split(jax.random.key(seed), 4)
    matrix = scatter_about(arg_keys[0], (ORDER, WCOLS), 1.0, 6.0, ((0, 8), (1, 32)))
    u_inverse = draw_u_inverse(jax.random.fold_in(arg_keys[3], 71), 0)
    l_inverse = draw_l_inverse(jax.random.fold_in(arg_keys[3], 71), 0)
    return dict(matrix=matrix, u_inverse=u_inverse, l_inverse=l_inverse)


def reference(matrix, u_inverse, l_inverse):
    stored = jnp.arange(ORDER) // NB
    row_ids = (stored % RB) * N_PROW + stored // RB
    col_ids = jnp.arange(WCOLS) // NB
    current = matrix
    for panel_id in range(PANELS):
        start = panel_id * NB
        head_start = panel_id * RB * NB
        panel = current[:, start:start + NB].astype(jnp.float32)
        lower = jnp.dot(panel, u_inverse[panel_id], precision=lax.Precision.HIGHEST).astype(jnp.bfloat16)
        lower = jnp.where(row_ids[:, None] > panel_id, lower, jnp.zeros_like(lower))
        head = current[head_start:head_start + NB].astype(jnp.float32)
        upper = jnp.dot(l_inverse[panel_id], head, precision=lax.Precision.HIGHEST).astype(jnp.bfloat16)
        upper = jnp.where(col_ids[None, :] > panel_id, upper, jnp.zeros_like(upper))

        def refresh(pair, upper=upper):
            block, left = pair
            product = jnp.dot(left, upper, preferred_element_type=jnp.float32)
            return (block.astype(jnp.float32) - product).astype(jnp.bfloat16)

        blocks = lax.map(refresh, (current.reshape(ORDER // NB, NB, WCOLS), lower.reshape(ORDER // NB, NB, NB)))
        current = blocks.reshape(ORDER, WCOLS)
        current = current.at[:, start:start + NB].set(
            jnp.where(row_ids[:, None] > panel_id, lower, current[:, start:start + NB]))
        current = current.at[head_start:head_start + NB].set(
            jnp.where(col_ids[None, :] > panel_id, upper, current[head_start:head_start + NB]))
    return current
```

```python
import functools

import jax
import jax.numpy as jnp
from jax import lax
from jax.experimental import pallas as pl
from jax.experimental.pallas import tpu as pltpu
from jax.sharding import PartitionSpec as P

NX, NZ = 4, 8
NB = 512
EXTRA = 32
CHUNKS = (112, 112)


def node(x, z):
    return (x % NX) * NZ + z % NZ


def shift(dx, dz):
    return [(node(x, z), node(x + dx, z + dz)) for x in range(NX) for z in range(NZ)]


def from_sources(x, k):
    return [(node(0, 0), node(x, -k)), (node(0, 1), node(x, 1 + k))]


def move(value, pairs):
    return lax.ppermute(value, "pcol", pairs)


def first_row(chunk, r, k):
    return 16 * sum(CHUNKS[:chunk]) + CHUNKS[chunk] * (2 * ((r % 2) * 4 + k) + r // 2)


def spread_heads(matrix):
    y = lax.axis_index("prow") // 2
    own = matrix[:NB]
    ahead = lax.ppermute(own, "prow", [(0, 2), (1, 3)])
    back = lax.ppermute(own, "prow", [(0, 6), (1, 7)])
    across = lax.ppermute(own, "prow", [(0, 4), (1, 5)])
    mine = jnp.where(y == 0, own, jnp.where(y == 1, ahead, jnp.where(y == 2, across, back)))
    other = lax.ppermute(mine, "prow", [(i, i ^ 1) for i in range(8)])
    return mine, other


def scatter(chunk, matrix, extra, x, k):
    rows = CHUNKS[chunk]

    def piece(r, kk):
        start = first_row(chunk, r, kk)
        part = matrix[start : start + rows]
        if extra is None:
            return [part]
        at = EXTRA * (r * 4 + kk)
        return [part, extra[at : at + EXTRA]]

    def pieces(*which):
        return jnp.concatenate([p for w in which for p in piece(*w)], 0)

    n = rows + (0 if extra is None else EXTRA)
    to_one = move(pieces(*[(1, kk) for kk in range(4)]), from_sources(1, 0))
    to_three = move(pieces(*[(3, kk) for kk in range(4)]), from_sources(3, 0))
    even = {kk: move(pieces((0, kk), (2, kk)), from_sources(0, kk)) for kk in (3, 2, 1)}
    held = jnp.where(x == 1, to_one, to_three)
    odd = {
        kk: move(
            held[kk * n : (kk + 1) * n],
            [pair for r in (1, 3) for pair in ((node(r, 0), node(r, -kk)), (node(r, 1), node(r, 1 + kk)))],
        )
        for kk in (3, 2, 1)
    }

    def choose(own, there):
        return jnp.where(k == 0, own, jnp.where(k == 1, there[1], jnp.where(k == 2, there[2], there[3])))

    single = choose(held[:n], odd)
    both = choose(pieces((0, 0), (2, 0)), even)
    sent = jnp.where(x == 0, both, jnp.concatenate([single, single], 0))
    came = move(sent, [(node(a, z), node(b, z)) for a, b in ((0, 2), (1, 3), (3, 1)) for z in range(NZ)])
    low = jnp.where(x == 0, both[:n], jnp.where(x == 1, single, came[:n]))
    high = jnp.where(x == 0, both[n:], jnp.where(x == 1, came[:n], jnp.where(x == 2, came[n:], single)))
    return jnp.concatenate([low, high], 0), n


def gather(double, n):
    got = [(double, 0, 0, 0, 2)]
    got.append((move(double[:n], shift(1, 0)), 1, 0, 0, 1))
    got.append((move(double[n:], shift(-1, 0)), 1, 0, 1, 1))
    up = down = double
    for s in range(1, 5):
        if s == 4:
            up, down = up[:n], down[n:]
        up, down = move(up, shift(0, 1)), move(down, shift(0, -1))
        halves, second = (2, 0) if s < 4 else (1, 1)
        got.append((up, 0, -s, 0, halves))
        got.append((down, 0, s, second, halves))
        got.append((move(up, shift(1, 0)), 1, -s, 0, halves))
        got.append((move(down, shift(-1, 0)), 1, s, second, halves))
    return got


def split(value):
    high = value.astype(jnp.bfloat16)
    return high, (value - high.astype(jnp.float32)).astype(jnp.bfloat16)


def dot(a, b):
    return jnp.dot(a, b, preferred_element_type=jnp.float32)


def factor_kernel(plan, ids, a_hbm, mine_hbm, other_hbm, u_hbm, l_hbm, *refs):
    count = len(plan)
    bufs, out_hbm = refs[:count], refs[count]
    (panels, extras, a, out, heads, inverse, u_hi, u_lo, l_hi, l_lo, uppers, sems, out_sems) = refs[count + 1 :]
    prow, pcol = ids[0], ids[1]
    core = prow % 2
    x, z = pcol // NZ, pcol % NZ
    blocks = a.shape[0] // NB
    used = [0]
    small, rest = [], []

    def start(src, dst, group):
        copy = pltpu.make_async_copy(src, dst, sems.at[used[0]])
        used[0] += 1
        copy.start()
        group.append(copy)

    start(u_hbm, inverse.at[0:2], small)
    start(l_hbm, inverse.at[2:4], small)
    start(mine_hbm, heads.at[core], small)
    start(other_hbm, heads.at[1 - core], small)
    for wanted in (small, rest):
        for buf, (chunk, n, dx, dz, first, halves) in zip(bufs, plan):
            zz = (z + dz + NZ) % NZ
            panel = jnp.where((zz >= 1) & (zz <= 4), 1, 0)
            k = jnp.where(panel == 1, zz - 1, (NZ - zz) % NZ)
            parity = (x + dx) % 2
            rows = CHUNKS[chunk]
            for i in range(halves):
                half = first + i
                if wanted is small:
                    if n > rows:
                        at = pl.multiple_of(EXTRA * ((parity + 2 * half) * 4 + k), 16)
                        start(buf.at[pl.ds(i * n + rows, EXTRA)], extras.at[panel, pl.ds(at, EXTRA)], small)
                else:
                    at = 16 * sum(CHUNKS[:chunk]) + rows * (2 * (parity * 4 + k) + half)
                    at = pl.multiple_of(at, 16)
                    start(buf.at[pl.ds(i * n, rows)], panels.at[panel, pl.ds(at, rows)], rest)
    start(a_hbm, a, rest)
    for copy in small:
        copy.wait()
    for p in range(2):
        u_hi[p], u_lo[p] = split(inverse[p])
        l_hi[p], l_lo[p] = split(inverse[2 + p])

    def lower(value, p):
        left = dot(value[:, : NB // 2], u_hi[p, : NB // 2, : NB // 2]) + dot(
            value[:, : NB // 2], u_lo[p, : NB // 2, : NB // 2]
        )
        right = dot(value, u_hi[p, :, NB // 2 :]) + dot(value, u_lo[p, :, NB // 2 :])
        return jnp.concatenate([left, right], 1).astype(jnp.bfloat16)

    def upper(value, p):
        return (dot(l_hi[p], value) + dot(l_lo[p], value)).astype(jnp.bfloat16)

    def minus(value, product):
        return (value.astype(jnp.float32) - product).astype(jnp.bfloat16)

    zero = jnp.zeros((NB, NB), jnp.bfloat16)
    uppers[0] = upper(extras[1], 0)
    uppers[1] = jnp.where(pcol > 0, upper(heads[0], 0), zero)
    head = minus(heads[1], dot(lower(extras[0], 0), uppers[1]))
    uppers[2] = jnp.where(pcol > 1, upper(head, 1), zero)
    for copy in rest:
        copy.wait()

    def block(s, carry):
        g = s * 8 + prow
        at = pl.ds(pl.multiple_of(s * NB, NB), NB)
        lower0 = jnp.where(g > 0, lower(panels[0, at], 0), zero)
        current = minus(a[at], dot(lower0, uppers[1]))
        column = minus(panels[1, at], dot(lower0, uppers[0]))
        lower1 = jnp.where(g > 1, lower(column, 1), zero)
        out[at] = minus(current, dot(lower1, uppers[2]))

        @pl.when((pcol == 0) & (g > 0))
        def _():
            out[at] = lower0

        @pl.when((pcol == 1) & (g > 1))
        def _():
            out[at] = lower1

        @pl.when((pcol > 0) & (g == 0))
        def _():
            out[at] = uppers[1]

        @pl.when((pcol > 1) & (g == 1))
        def _():
            out[at] = uppers[2]

        pltpu.make_async_copy(out.at[at], out_hbm.at[at], out_sems.at[s]).start()
        return carry

    lax.fori_loop(0, blocks, block, 0)
    for s in range(blocks):
        at = pl.ds(s * NB, NB)
        pltpu.make_async_copy(out.at[at], out_hbm.at[at], out_sems.at[s]).wait()


def factor(matrix, mine, other, u_inverse, l_inverse, got, ids):
    rows = matrix.shape[0]
    plan = tuple((chunk, n, dx, dz, first, halves) for chunk, n, (_, dx, dz, first, halves) in got)
    bufs = [entry[0] for _, _, entry in got]
    copies = 5 + sum(p[5] * (2 if p[1] > CHUNKS[p[0]] else 1) for p in plan)
    hbm = pl.BlockSpec(memory_space=pl.ANY)
    square = (2, NB, NB)
    return pl.pallas_call(
        functools.partial(factor_kernel, plan),
        out_shape=jax.ShapeDtypeStruct(matrix.shape, matrix.dtype),
        in_specs=[pl.BlockSpec(memory_space=pltpu.SMEM)] + [hbm] * (5 + len(bufs)),
        out_specs=hbm,
        scratch_shapes=[
            pltpu.VMEM((2, rows, NB), jnp.bfloat16),
            pltpu.VMEM(square, jnp.bfloat16),
            pltpu.VMEM((rows, NB), jnp.bfloat16),
            pltpu.VMEM((rows, NB), jnp.bfloat16),
            pltpu.VMEM(square, jnp.bfloat16),
            pltpu.VMEM((4, NB, NB), jnp.float32),
            pltpu.VMEM(square, jnp.bfloat16),
            pltpu.VMEM(square, jnp.bfloat16),
            pltpu.VMEM(square, jnp.bfloat16),
            pltpu.VMEM(square, jnp.bfloat16),
            pltpu.VMEM((3, NB, NB), jnp.bfloat16),
            pltpu.SemaphoreType.DMA((copies,)),
            pltpu.SemaphoreType.DMA((rows // NB,)),
        ],
        compiler_params=pltpu.CompilerParams(vmem_limit_bytes=48 * 1024 * 1024),
        cost_estimate=pl.CostEstimate(flops=12 * rows * NB * NB, bytes_accessed=8 * rows * NB, transcendentals=0),
    )(ids, matrix, mine, other, u_inverse, l_inverse, *bufs)


def body(matrix, u_inverse, l_inverse):
    prow, pcol = lax.axis_index("prow"), lax.axis_index("pcol")
    core = prow % 2
    x, z = pcol // NZ, pcol % NZ
    k = jnp.where((z >= 1) & (z <= 4), z - 1, (NZ - z) % NZ)
    mine, other = spread_heads(matrix)
    extra = jnp.where((pcol == 0) == (core == 1), mine, other)
    got = []
    for chunk in range(len(CHUNKS)):
        last = chunk == len(CHUNKS) - 1
        double, n = scatter(chunk, matrix, extra if last else None, x, k)
        got += [(chunk, n, entry) for entry in gather(double, n)]
    ids = jnp.stack([prow, pcol]).astype(jnp.int32)
    return factor(matrix, mine, other, u_inverse, l_inverse, got, ids)


def solution(mesh):
    in_specs = (P("prow", "pcol"), P(), P())
    return jax.shard_map(body, mesh=mesh, in_specs=in_specs, out_specs=P("prow", "pcol"), check_vma=False)
```

```python
import functools

import jax
import jax.numpy as jnp
from jax import lax
from jax.experimental import pallas as pl
from jax.experimental.pallas import tpu as pltpu
from jax.sharding import PartitionSpec as P

NX, NZ = 4, 8
NB = 512
N = 224


def node(x, z):
    return (x % NX) * NZ + z % NZ


def shift(dx, dz):
    return [(node(x, z), node(x + dx, z + dz)) for x in range(NX) for z in range(NZ)]


def from_sources(x, k):
    return [(node(0, 0), node(x, -k)), (node(0, 1), node(x, 1 + k))]


def move(value, pairs):
    return lax.ppermute(value, "pcol", pairs)


def tie(*values):
    return lax.optimization_barrier(values)


def first_row(parity, k, half):
    return 2 * N * k + N * half if parity == 0 else 8 * N + 4 * N * half + N * k


def beside_y(own):
    y = lax.axis_index("prow") // 2
    ahead = lax.ppermute(own, "prow", [(0, 2), (1, 3)])
    back = lax.ppermute(own, "prow", [(0, 6), (1, 7)])
    return jnp.where(y == 1, ahead, jnp.where(y == 3, back, own))


def across_y(own):
    y = lax.axis_index("prow") // 2
    half = own.shape[0] // 2
    low = lax.ppermute(own[:half], "prow", [(2, 4), (3, 5)])
    high = lax.ppermute(own[half:], "prow", [(6, 4), (7, 5)])
    return jnp.where(y == 2, jnp.concatenate([low, high], 0), own)


def swap_cores(value):
    return lax.ppermute(value, "prow", [(i, i ^ 1) for i in range(8)])


def grow(value, stage, x, z, core):
    def send(hops):
        pairs = [
            (NX * NZ * prow + node(a[0], a[1] + 1 - prow), NX * NZ * prow + node(b[0], b[1] + 1 - prow))
            for prow in (0, 1)
            for a, b in hops
        ]
        return lax.ppermute(value, ("prow", "pcol"), pairs)

    c = (z - 1 + core + NZ) % NZ
    if stage == 0:
        two, six, four = (send([((0, 0), (0, d))]) for d in (2, 6, 4))
        there = jnp.where(c == 2, two, jnp.where(c == 6, six, four))
        return jnp.where((x == 0) & (c % 2 == 0) & (c > 0), there, value)
    if stage == 1:
        one, three, two = (send([((0, d), (r, d)) for d in (0, 2, 4, 6)]) for r in (1, 3, 2))
        there = jnp.where(x == 1, one, jnp.where(x == 3, three, two))
        return jnp.where((x > 0) & (c % 2 == 0), there, value)
    return jnp.where(c % 2 == 1, send([((r, d), (r, d + 1)) for r in range(NX) for d in (0, 2, 4, 6)]), value)


def exchange(matrix, x, z, k, core, make_weights):
    block = matrix[:NB]
    parts = tie(*[matrix[2 * N * kk : 2 * N * (kk + 1)] for kk in (1, 2, 3)], matrix)
    even = [move(parts[kk - 1], from_sources(0, kk)) for kk in (1, 2, 3)]
    one = move(parts[3][8 * N : 12 * N], from_sources(1, 0))
    three = move(parts[3][12 * N : 16 * N], from_sources(3, 0))

    def along(value, kk):
        return move(value, [p for r in (1, 3) for p in ((node(r, 0), node(r, -kk)), (node(r, 1), node(r, 1 + kk)))])

    one, three, *even = tie(one, three, *even)
    held = jnp.where(x == 1, one, three)
    odd = [along(held[N * kk : N * (kk + 1)], kk) for kk in (1, 2, 3)]
    extra = grow(block, 0, x, z, core)

    def choose(own, one, two, three):
        return jnp.where(k == 0, own, jnp.where(k == 1, one, jnp.where(k == 2, two, three)))

    single = choose(held[:N], *odd)
    both = choose(matrix[: 2 * N], *even)
    sent = jnp.where(x == 0, both, jnp.concatenate([single, single], 0))
    sent, extra = tie(sent, extra)
    came = move(sent, [(node(a, c), node(b, c)) for a, b in ((0, 2), (1, 3), (3, 1)) for c in range(NZ)])
    extra = grow(extra, 1, x, z, core)
    first = jnp.where(x == 3, came[:N], sent[:N])
    second = jnp.where(x == 1, came[:N], sent[N:])
    double = jnp.where(x == 2, came, jnp.concatenate([first, second], 0))

    double, extra = tie(double, extra)
    near_rows, far_rows = [(double, 0, 0, 0, 2)], []
    up = down = double
    xup, xdown = double[:N], double[N:]
    carried = (extra,)
    for s in range(1, 5):
        if s == 4:
            up, down = up[:N], down[N:]
        dz = s - 1
        up, down = move(up, shift(0, 1)), move(down, shift(0, -1))
        xup, xdown = move(xup, shift(1, 0)), move(xdown, shift(-1, 0))
        if s == 1:
            carried = (jnp.concatenate([block, grow(carried[0], 2, x, z, core)], 0),)
        elif s == 2:
            carried = make_weights(carried[0], swap_cores(carried[0]))
        elif s == 3:
            carried = (beside_y(carried[0]), carried[1])
        else:
            carried = (across_y(carried[0]), carried[1])
        up, down, xup, xdown, *carried = tie(up, down, xup, xdown, *carried)
        whole = 2 if 1 < s else 1
        far_rows.append((xup, 1, -dz, 0, whole))
        far_rows.append((xdown, 1, dz, 1 if s == 1 else 0, whole))
        near_rows.append((up, 0, -s, 0, 2 if s < 4 else 1))
        near_rows.append((down, 0, s, 0 if s < 4 else 1, 2 if s < 4 else 1))
        xup, xdown = up, down
    far_rows.append((move(xup, shift(1, 0)), 1, -4, 0, 1))
    far_rows.append((move(xdown, shift(-1, 0)), 1, 4, 1, 1))
    weights, top = carried
    return near_rows, far_rows, (weights, swap_cores(weights)), top


def dot(a, b):
    return jnp.dot(a, b, preferred_element_type=jnp.float32)


def split(value):
    big = value * 65537.0
    high = big - (big - value)
    return high.astype(jnp.bfloat16), (value - high).astype(jnp.bfloat16)


def accurate(a, b):
    if isinstance(a, tuple) and isinstance(b, tuple):
        return dot(a[0], b[0]) + dot(a[0], b[1]) + dot(a[1], b[0])
    if isinstance(a, tuple):
        return dot(a[0], b) + dot(a[1], b)
    return dot(a, b[0]) + dot(a, b[1])


def weights_kernel(ids, mine, other, u, l, weights, top):
    prow, pcol = ids[0], ids[1]
    even = prow % 2 == 0
    head0, right = jnp.where(even, mine[:NB], other[:NB]), jnp.where(even, mine[NB:], other[NB:])
    head1, below = jnp.where(even, other[:NB], mine[:NB]), jnp.where(even, other[NB:], mine[NB:])
    u0, u1, l0, l1 = split(u[0]), split(u[1]), split(l[0]), split(l[1])
    upper01 = accurate(l0, right).astype(jnp.bfloat16)
    upper0 = accurate(l0, head0).astype(jnp.bfloat16)
    lower = accurate(below, u0).astype(jnp.bfloat16)
    step = jnp.where(pcol > 0, dot(lower, upper0), 0.0)
    fresh = (head1.astype(jnp.float32) - step).astype(jnp.bfloat16)
    upper1 = accurate(l1, fresh).astype(jnp.bfloat16)
    second = jnp.where(pcol > 1, accurate(u1, upper1), jnp.where(pcol == 1, -u[1], 0.0))
    row = lax.broadcasted_iota(jnp.int32, (NB, NB), 0)
    col = lax.broadcasted_iota(jnp.int32, (NB, NB), 1)
    minus_one = jnp.where((row == col) & (pcol == 0), -1.0, 0.0)
    base = jnp.where(pcol > 1, upper0.astype(jnp.float32), minus_one)
    first = accurate(u0, split(base - accurate(upper01, split(second))))
    weights[...] = jnp.where(even, first, second).astype(jnp.bfloat16)
    top0 = jnp.where(pcol > 0, upper0, head0)
    top1 = jnp.where(pcol > 1, upper1, jnp.where(pcol == 1, fresh, lower))
    top[...] = jnp.where(prow == 0, top0, top1)


def make_weights(ids, heads, others, u_inverse, l_inverse):
    vmem = pl.BlockSpec(memory_space=pltpu.VMEM)
    return pl.pallas_call(
        weights_kernel,
        out_shape=(
            jax.ShapeDtypeStruct((NB, NB), jnp.bfloat16),
            jax.ShapeDtypeStruct((NB, NB), jnp.bfloat16),
        ),
        in_specs=[pl.BlockSpec(memory_space=pltpu.SMEM)] + [vmem] * 4,
        out_specs=(vmem, vmem),
        compiler_params=pltpu.CompilerParams(vmem_limit_bytes=48 * 1024 * 1024),
        cost_estimate=pl.CostEstimate(flops=34 * NB**3, bytes_accessed=16 * NB * NB, transcendentals=0),
    )(ids, heads, others, u_inverse, l_inverse)


def factor_kernel(plan, part, ids, a_hbm, mine_hbm, other_hbm, top_hbm, *refs):
    count = len(plan)
    bufs, out_hbm = refs[:count], refs[-8]
    panels, a, out, w, top, sems, out_sems = refs[-7:]
    prow, pcol = ids[0], ids[1]
    x, z = pcol // NZ, pcol % NZ
    parity = (x + part) % 2
    rows = a.shape[0]
    base = pl.multiple_of(parity * rows, 16)
    slots = 16
    copies = []

    def start(src, dst):
        copy = pltpu.make_async_copy(src, dst, sems.at[slots + len(copies)])
        copy.start()
        copies.append(copy)

    core = prow % 2
    start(mine_hbm, w.at[pl.ds(pl.multiple_of(core * NB, NB), NB)])
    start(other_hbm, w.at[pl.ds(pl.multiple_of((1 - core) * NB, NB), NB)])
    start(a_hbm.at[pl.ds(base, rows)], a)
    start(top_hbm, top)

    def landing(panel, k, half):
        at = jnp.where(parity == 0, first_row(0, k, half), first_row(1, k, half) - rows)
        return panels.at[panel, pl.ds(pl.multiple_of(at, 16), N)], sems.at[8 * panel + 2 * k + half]

    for buf, (_, dz, first, halves) in zip(bufs, plan):
        zz = (z + dz + NZ) % NZ
        panel = jnp.where((zz >= 1) & (zz <= 4), 1, 0)
        k = jnp.where(panel == 1, zz - 1, (NZ - zz) % NZ)
        for i in range(halves):
            dst, sem = landing(panel, k, first + i)
            pltpu.make_async_copy(buf.at[pl.ds(i * N, N)], dst, sem).start()
    for copy in copies:
        copy.wait()
    size = 2 * N
    for s in range(rows // size):
        at = pl.ds(s * size, size)
        for panel in range(2):
            for i in range(2):
                k = jnp.where(parity == 0, s, 2 * (s % 2) + i)
                half = jnp.where(parity == 0, i, s // 2)
                dst, sem = landing(panel, k, half)
                pltpu.make_async_copy(bufs[0].at[pl.ds(0, N)], dst, sem).wait()
        product = dot(panels[0, at], w[:NB]) + dot(panels[1, at], w[NB:])
        value = jnp.where(pcol > 1, a[at].astype(jnp.float32), 0.0)
        out[at] = (value - product).astype(jnp.bfloat16)
        if s == 0:

            @pl.when((parity == 0) & (prow < 2))
            def _():
                out[:size] = top[:size]

        if s == 1:

            @pl.when((parity == 0) & (prow < 2))
            def _():
                out[size:NB] = top[size:]

        to = pl.ds(pl.multiple_of(base + s * size, 16), size)
        pltpu.make_async_copy(out.at[at], out_hbm.at[to], out_sems.at[s]).start()
    for s in range(rows // size):
        at = pl.ds(s * size, size)
        to = pl.ds(pl.multiple_of(base + s * size, 16), size)
        pltpu.make_async_copy(out.at[at], out_hbm.at[to], out_sems.at[s]).wait()


def factor(part, ids, matrix, weights, top, got, result=None):
    rows = matrix.shape[0] // 2
    plan = tuple(entry[1:] for entry in got)
    operands = [ids, matrix, *weights, top] + [entry[0] for entry in got] + ([] if result is None else [result])
    hbm = pl.BlockSpec(memory_space=pl.ANY)
    return pl.pallas_call(
        functools.partial(factor_kernel, plan, part),
        out_shape=jax.ShapeDtypeStruct(matrix.shape, matrix.dtype),
        in_specs=[pl.BlockSpec(memory_space=pltpu.SMEM)] + [hbm] * (len(operands) - 1),
        out_specs=hbm,
        input_output_aliases={} if result is None else {len(operands) - 1: 0},
        scratch_shapes=[
            pltpu.VMEM((2, rows, NB), jnp.bfloat16),
            pltpu.VMEM((rows, NB), jnp.bfloat16),
            pltpu.VMEM((rows, NB), jnp.bfloat16),
            pltpu.VMEM((2 * NB, NB), jnp.bfloat16),
            pltpu.VMEM((NB, NB), jnp.bfloat16),
            pltpu.SemaphoreType.DMA((20,)),
            pltpu.SemaphoreType.DMA((rows // (2 * N),)),
        ],
        compiler_params=pltpu.CompilerParams(vmem_limit_bytes=56 * 1024 * 1024),
        cost_estimate=pl.CostEstimate(flops=4 * rows * NB * NB, bytes_accessed=8 * rows * NB, transcendentals=0),
    )(*operands)


def body(matrix, u_inverse, l_inverse):
    prow, pcol = lax.axis_index("prow"), lax.axis_index("pcol")
    x, z = pcol // NZ, pcol % NZ
    k = jnp.where((z >= 1) & (z <= 4), z - 1, (NZ - z) % NZ)
    ids = jnp.stack([prow, pcol]).astype(jnp.int32)
    near_rows, far_rows, weights, top = exchange(
        matrix, x, z, k, prow % 2, lambda mine, other: make_weights(ids, mine, other, u_inverse, l_inverse)
    )
    half = factor(0, ids, matrix, weights, top, near_rows)
    return factor(1, ids, matrix, weights, top, far_rows, half)


def solution(mesh):
    in_specs = (P("prow", "pcol"), P(), P())
    return jax.shard_map(body, mesh=mesh, in_specs=in_specs, out_specs=P("prow", "pcol"), check_vma=False)
```

```python
import functools

import jax
import jax.numpy as jnp
from jax import lax
from jax.experimental import pallas as pl
from jax.experimental.pallas import tpu as pltpu
from jax.sharding import PartitionSpec as P

NX, NZ = 4, 8
NB = 512
N = 224


def node(x, z):
    return (x % NX) * NZ + z % NZ


def shift(dx, dz):
    return [(node(x, z), node(x + dx, z + dz)) for x in range(NX) for z in range(NZ)]


def from_sources(x, k):
    return [(node(0, 0), node(x, -k)), (node(0, 1), node(x, 1 + k))]


def move(value, pairs):
    return lax.ppermute(value, "pcol", pairs)


def tie(*values):
    return lax.optimization_barrier(values)


def first_row(parity, k, half):
    return 2 * N * k + N * half if parity == 0 else 8 * N + 4 * N * half + N * k


def along_y(own):
    y = lax.axis_index("prow") // 2
    ahead = lax.ppermute(own, "prow", [(0, 2), (1, 3)])
    back = lax.ppermute(own, "prow", [(0, 6), (1, 7)])
    across = lax.ppermute(own, "prow", [(0, 4), (1, 5)])
    return jnp.where(y == 0, own, jnp.where(y == 1, ahead, jnp.where(y == 2, across, back)))


def swap_cores(value):
    return lax.ppermute(value, "prow", [(i, i ^ 1) for i in range(8)])


def grow(value, stage, x, z, core):
    def send(hops):
        pairs = [
            (NX * NZ * prow + node(a[0], a[1] + 1 - prow), NX * NZ * prow + node(b[0], b[1] + 1 - prow))
            for prow in (0, 1)
            for a, b in hops
        ]
        return lax.ppermute(value, ("prow", "pcol"), pairs)

    c = (z - 1 + core + NZ) % NZ
    if stage == 0:
        two, six, four = (send([((0, 0), (0, d))]) for d in (2, 6, 4))
        there = jnp.where(c == 2, two, jnp.where(c == 6, six, four))
        return jnp.where((x == 0) & (c % 2 == 0) & (c > 0), there, value)
    if stage == 1:
        one, three, two = (send([((0, d), (r, d)) for d in (0, 2, 4, 6)]) for r in (1, 3, 2))
        there = jnp.where(x == 1, one, jnp.where(x == 3, three, two))
        return jnp.where((x > 0) & (c % 2 == 0), there, value)
    return jnp.where(c % 2 == 1, send([((r, d), (r, d + 1)) for r in range(NX) for d in (0, 2, 4, 6)]), value)


def exchange(matrix, x, z, k, core, make_weights):
    block = matrix[:NB]
    parts = tie(*[matrix[2 * N * kk : 2 * N * (kk + 1)] for kk in (1, 2, 3)], matrix)
    even = [move(parts[kk - 1], from_sources(0, kk)) for kk in (1, 2, 3)]
    one = move(parts[3][8 * N : 12 * N], from_sources(1, 0))
    three = move(parts[3][12 * N : 16 * N], from_sources(3, 0))

    def along(value, kk):
        return move(value, [p for r in (1, 3) for p in ((node(r, 0), node(r, -kk)), (node(r, 1), node(r, 1 + kk)))])

    one, three, *even = tie(one, three, *even)
    held = jnp.where(x == 1, one, three)
    odd = [along(held[N * kk : N * (kk + 1)], kk) for kk in (1, 2, 3)]
    extra = grow(block, 0, x, z, core)

    def choose(own, one, two, three):
        return jnp.where(k == 0, own, jnp.where(k == 1, one, jnp.where(k == 2, two, three)))

    single = choose(held[:N], *odd)
    both = choose(matrix[: 2 * N], *even)
    sent = jnp.where(x == 0, both, jnp.concatenate([single, single], 0))
    came = move(sent, [(node(a, c), node(b, c)) for a, b in ((0, 2), (1, 3), (3, 1)) for c in range(NZ)])
    extra = grow(extra, 1, x, z, core)
    first = jnp.where(x == 3, came[:N], sent[:N])
    second = jnp.where(x == 1, came[:N], sent[N:])
    double = jnp.where(x == 2, came, jnp.concatenate([first, second], 0))

    near_rows, far_rows = [(double, 0, 0, 0, 2)], []
    up = down = double
    xup, xdown = double[:N], double[N:]
    carried = (extra,)
    for s in range(1, 5):
        if s == 4:
            up, down = up[:N], down[N:]
        dz = s - 1
        up, down = move(up, shift(0, 1)), move(down, shift(0, -1))
        xup, xdown = move(xup, shift(1, 0)), move(xdown, shift(-1, 0))
        if s == 1:
            carried = (jnp.concatenate([block, grow(carried[0], 2, x, z, core)], 0),)
        elif s == 2:
            carried = make_weights(carried[0], swap_cores(carried[0]))
        elif s == 4:
            carried = (weights, top)
        up, down, xup, xdown, *carried = tie(up, down, xup, xdown, *carried)
        if s == 2:
            weights, top = along_y(carried[0]), carried[1]
            carried = ()
        whole = 2 if 1 < s else 1
        far_rows.append((xup, 1, -dz, 0, whole))
        far_rows.append((xdown, 1, dz, 1 if s == 1 else 0, whole))
        near_rows.append((up, 0, -s, 0, 2 if s < 4 else 1))
        near_rows.append((down, 0, s, 0 if s < 4 else 1, 2 if s < 4 else 1))
        xup, xdown = up, down
    far_rows.append((move(xup, shift(1, 0)), 1, -4, 0, 1))
    far_rows.append((move(xdown, shift(-1, 0)), 1, 4, 1, 1))
    weights, top = carried
    return near_rows, far_rows, (weights, swap_cores(weights)), top


def dot(a, b):
    return jnp.dot(a, b, preferred_element_type=jnp.float32)


def split(value):
    big = value * 65537.0
    high = big - (big - value)
    return high.astype(jnp.bfloat16), (value - high).astype(jnp.bfloat16)


def accurate(a, b):
    if isinstance(a, tuple) and isinstance(b, tuple):
        return dot(a[0], b[0]) + dot(a[0], b[1]) + dot(a[1], b[0])
    if isinstance(a, tuple):
        return dot(a[0], b) + dot(a[1], b)
    return dot(a, b[0]) + dot(a, b[1])


def weights_kernel(ids, mine, other, u, l, weights, top):
    prow, pcol = ids[0], ids[1]
    even = prow % 2 == 0
    head0, right = jnp.where(even, mine[:NB], other[:NB]), jnp.where(even, mine[NB:], other[NB:])
    head1, below = jnp.where(even, other[:NB], mine[:NB]), jnp.where(even, other[NB:], mine[NB:])
    u0, u1, l0, l1 = split(u[0]), split(u[1]), split(l[0]), split(l[1])
    upper01 = accurate(l0, right).astype(jnp.bfloat16)
    upper0 = accurate(l0, head0).astype(jnp.bfloat16)
    lower = accurate(below, u0).astype(jnp.bfloat16)
    step = jnp.where(pcol > 0, dot(lower, upper0), 0.0)
    fresh = (head1.astype(jnp.float32) - step).astype(jnp.bfloat16)
    upper1 = accurate(l1, fresh).astype(jnp.bfloat16)
    second = jnp.where(pcol > 1, accurate(u1, upper1), jnp.where(pcol == 1, -u[1], 0.0))
    row = lax.broadcasted_iota(jnp.int32, (NB, NB), 0)
    col = lax.broadcasted_iota(jnp.int32, (NB, NB), 1)
    minus_one = jnp.where((row == col) & (pcol == 0), -1.0, 0.0)
    base = jnp.where(pcol > 1, upper0.astype(jnp.float32), minus_one)
    first = accurate(u0, split(base - accurate(upper01, split(second))))
    weights[...] = jnp.where(even, first, second).astype(jnp.bfloat16)
    top0 = jnp.where(pcol > 0, upper0, head0)
    top1 = jnp.where(pcol > 1, upper1, jnp.where(pcol == 1, fresh, lower))
    top[...] = jnp.where(prow == 0, top0, top1)


def make_weights(ids, heads, others, u_inverse, l_inverse):
    vmem = pl.BlockSpec(memory_space=pltpu.VMEM)
    return pl.pallas_call(
        weights_kernel,
        out_shape=(
            jax.ShapeDtypeStruct((NB, NB), jnp.bfloat16),
            jax.ShapeDtypeStruct((NB, NB), jnp.bfloat16),
        ),
        in_specs=[pl.BlockSpec(memory_space=pltpu.SMEM)] + [vmem] * 4,
        out_specs=(vmem, vmem),
        compiler_params=pltpu.CompilerParams(vmem_limit_bytes=48 * 1024 * 1024),
        cost_estimate=pl.CostEstimate(flops=34 * NB**3, bytes_accessed=16 * NB * NB, transcendentals=0),
    )(ids, heads, others, u_inverse, l_inverse)


def factor_kernel(plan, part, ids, a_hbm, mine_hbm, other_hbm, top_hbm, *refs):
    count = len(plan)
    bufs, out_hbm = refs[:count], refs[-8]
    panels, a, out, w, top, sems, out_sems = refs[-7:]
    prow, pcol = ids[0], ids[1]
    x, z = pcol // NZ, pcol % NZ
    parity = (x + part) % 2
    rows = a.shape[0]
    base = pl.multiple_of(parity * rows, 16)
    slots = 16
    copies = []

    def start(src, dst):
        copy = pltpu.make_async_copy(src, dst, sems.at[slots + len(copies)])
        copy.start()
        copies.append(copy)

    core = prow % 2
    start(mine_hbm, w.at[pl.ds(pl.multiple_of(core * NB, NB), NB)])
    start(other_hbm, w.at[pl.ds(pl.multiple_of((1 - core) * NB, NB), NB)])
    start(a_hbm.at[pl.ds(base, rows)], a)
    start(top_hbm, top)

    def landing(panel, k, half):
        at = jnp.where(parity == 0, first_row(0, k, half), first_row(1, k, half) - rows)
        return panels.at[panel, pl.ds(pl.multiple_of(at, 16), N)], sems.at[8 * panel + 2 * k + half]

    for buf, (_, dz, first, halves) in zip(bufs, plan):
        zz = (z + dz + NZ) % NZ
        panel = jnp.where((zz >= 1) & (zz <= 4), 1, 0)
        k = jnp.where(panel == 1, zz - 1, (NZ - zz) % NZ)
        for i in range(halves):
            dst, sem = landing(panel, k, first + i)
            pltpu.make_async_copy(buf.at[pl.ds(i * N, N)], dst, sem).start()
    for copy in copies:
        copy.wait()
    size = 2 * N
    for s in range(rows // size):
        at = pl.ds(s * size, size)
        for panel in range(2):
            for i in range(2):
                k = jnp.where(parity == 0, s, 2 * (s % 2) + i)
                half = jnp.where(parity == 0, i, s // 2)
                dst, sem = landing(panel, k, half)
                pltpu.make_async_copy(bufs[0].at[pl.ds(0, N)], dst, sem).wait()
        product = dot(panels[0, at], w[:NB]) + dot(panels[1, at], w[NB:])
        value = jnp.where(pcol > 1, a[at].astype(jnp.float32), 0.0)
        out[at] = (value - product).astype(jnp.bfloat16)
        if s == 0:

            @pl.when((parity == 0) & (prow < 2))
            def _():
                out[:size] = top[:size]

        if s == 1:

            @pl.when((parity == 0) & (prow < 2))
            def _():
                out[size:NB] = top[size:]

        to = pl.ds(pl.multiple_of(base + s * size, 16), size)
        pltpu.make_async_copy(out.at[at], out_hbm.at[to], out_sems.at[s]).start()
    for s in range(rows // size):
        at = pl.ds(s * size, size)
        to = pl.ds(pl.multiple_of(base + s * size, 16), size)
        pltpu.make_async_copy(out.at[at], out_hbm.at[to], out_sems.at[s]).wait()


def factor(part, ids, matrix, weights, top, got, result=None):
    rows = matrix.shape[0] // 2
    plan = tuple(entry[1:] for entry in got)
    operands = [ids, matrix, *weights, top] + [entry[0] for entry in got] + ([] if result is None else [result])
    hbm = pl.BlockSpec(memory_space=pl.ANY)
    return pl.pallas_call(
        functools.partial(factor_kernel, plan, part),
        out_shape=jax.ShapeDtypeStruct(matrix.shape, matrix.dtype),
        in_specs=[pl.BlockSpec(memory_space=pltpu.SMEM)] + [hbm] * (len(operands) - 1),
        out_specs=hbm,
        input_output_aliases={} if result is None else {len(operands) - 1: 0},
        scratch_shapes=[
            pltpu.VMEM((2, rows, NB), jnp.bfloat16),
            pltpu.VMEM((rows, NB), jnp.bfloat16),
            pltpu.VMEM((rows, NB), jnp.bfloat16),
            pltpu.VMEM((2 * NB, NB), jnp.bfloat16),
            pltpu.VMEM((NB, NB), jnp.bfloat16),
            pltpu.SemaphoreType.DMA((20,)),
            pltpu.SemaphoreType.DMA((rows // (2 * N),)),
        ],
        compiler_params=pltpu.CompilerParams(vmem_limit_bytes=56 * 1024 * 1024),
        cost_estimate=pl.CostEstimate(flops=4 * rows * NB * NB, bytes_accessed=8 * rows * NB, transcendentals=0),
    )(*operands)


def body(matrix, u_inverse, l_inverse):
    prow, pcol = lax.axis_index("prow"), lax.axis_index("pcol")
    x, z = pcol // NZ, pcol % NZ
    k = jnp.where((z >= 1) & (z <= 4), z - 1, (NZ - z) % NZ)
    ids = jnp.stack([prow, pcol]).astype(jnp.int32)
    near_rows, far_rows, weights, top = exchange(
        matrix, x, z, k, prow % 2, lambda mine, other: make_weights(ids, mine, other, u_inverse, l_inverse)
    )
    half = factor(0, ids, matrix, weights, top, near_rows)
    return factor(1, ids, matrix, weights, top, far_rows, half)


def solution(mesh):
    in_specs = (P("prow", "pcol"), P(), P())
    return jax.shard_map(body, mesh=mesh, in_specs=in_specs, out_specs=P("prow", "pcol"), check_vma=False)
```
